512 devices in a mesh: blk: 64 (over y, z_hi, x), rep: 8 (over z_lo, core).
Axes of the slice: x: 4, y: 8, z: 8 (z_hi: 2, z_lo: 4; z = z_hi * 4 + z_lo), core: 2. Of those that a mesh axis runs over, the one named last changes fastest.
Arguments:
- coords: float32 [3, 65536], P(None, 'blk'), may hold values from 0 to 12, as said below
- noise: float32 [65536], P('blk'), may hold values from 0.2 to 2
- right_side: float32 [4, 65536], P(None, 'blk'), may hold values from -8 to 8
Outputs:
- solution: float32 [4, 65536], P(None, 'blk')
- residual: float32 [4, 65536], P(None, 'blk')
The draws below stay inside these ranges and needn't reach their ends.
Inputs may be any that keep to these rules, and one draw needn't show every extreme that they name: `coords`: the first coordinate lies in [0, 12), the other two in [0, 4).
All inputs are finite; a program needn't handle non-finite values.
Results may differ from the reference program's by a relative error of at most 0.0003.
Values sent between devices are 32-bit elements; how exact they have to be, the bound alone decides.
A program may use at most 64 MiB of HBM per device.

```python
import math
import jax
import jax.numpy as jnp
from jax import lax

RHS = 4
ITERS = 2
TOTAL = 65536


def draw_coords(key, part):
    key = jax.random.fold_in(key, 11)
    key_along, key_across = jax.random.split(key)
    along = jax.random.uniform(key_along, (1, TOTAL), jnp.float32) * 12.0
    across = 4.0 * jax.random.uniform(key_across, (2, TOTAL), jnp.float32)
    return jnp.concatenate([along, across], axis=0).astype(jnp.float32)


def draw_right_side(key, part):
    key = jax.random.fold_in(key, 23)
    ramp = 0.6 + 1.2 * jnp.arange(TOTAL, dtype=jnp.float32) / TOTAL
    values = jax.random.truncated_normal(key, -4.0, 4.0, (RHS, TOTAL), jnp.float32)
    return (values * ramp[None, :]).astype(jnp.float32)


def levels(rng, dims, cuts, least, largest):
    loudness = 1.0
    for axis_at, parts in cuts:
        heights = jax.random.uniform(jax.random.fold_in(jax.random.fold_in(rng, 6), axis_at), (parts,), jnp.float32, least / len(cuts), largest / len(cuts))
        loudness = loudness * jnp.repeat(jnp.exp(heights), dims[axis_at] // parts).reshape((-1,) + (1,) * (len(dims) - 1 - axis_at))
    return loudness


def setup_inputs(seed: int = 0) -> dict:
    arg_keys = jax.random.split(jax.random.key(seed), 4)
    coords = draw_coords(jax.random.fold_in(arg_keys[3], 71), 0)
    noise = jnp.clip(jnp.exp(math.log(2.0) - 2.3025851 * jax.random.uniform(arg_keys[1], (TOTAL,), jnp.float32) ** levels(arg_keys[1], (TOTAL,), ((0, 64),), -0.2, 0.2)), 0.2, 2.0)
    right_side = draw_right_side(jax.random.fold_in(arg_keys[3], 71), 0)
    return dict(coords=coords, noise=noise, right_side=right_side)


def matern(dist_sq):
    scaled = jnp.sqrt(5.0 * dist_sq)
    return (1.0 + scaled + scaled * scaled / 3.0) * jnp.exp(-scaled)

def kernel_times(coords, vector, noise):
    width = min(256, TOTAL)
    count = TOTAL // width
    column_sets = coords.reshape(3, count, width).transpose(1, 0, 2)

    def one_set(columns):
        dist_sq = jnp.zeros((TOTAL, width), jnp.float32)
        for c in range(3):
            diff = coords[c][:, None] - columns[c][None, :]
            dist_sq = dist_sq + diff * diff
        kernel = matern(dist_sq)
        return jnp.dot(vector, kernel, precision=lax.Precision.HIGHEST, preferred_element_type=jnp.float32)
    images = lax.map(one_set, column_sets)
    return images.transpose(1, 0, 2).reshape(vector.shape[0], TOTAL) + noise[None, :] * vector

def reference(coords, noise, right_side):
    solution = jnp.zeros_like(right_side)
    residual = right_side
    direction = right_side
    norm_now = lax.optimization_barrier(jnp.sum(residual * residual, axis=1))
    for step in range(ITERS):
        image = kernel_times(coords, direction, noise)
        alpha = norm_now / lax.optimization_barrier(jnp.sum(direction * image, axis=1))
        solution = solution + alpha[:, None] * direction
        residual = residual - alpha[:, None] * image
        norm_next = lax.optimization_barrier(jnp.sum(residual * residual, axis=1))
        direction = residual + (norm_next / norm_now)[:, None] * direction
        norm_now = norm_next
    return (solution, residual)
```

```python
import functools
import math

import jax
import jax.numpy as jnp
from jax import lax
from jax.experimental import pallas as pl
from jax.experimental.pallas import tpu as pltpu
from jax.sharding import PartitionSpec as P

F32 = jnp.float32
BF16 = jnp.bfloat16
MESH = pl.DeviceIdType.MESH

LN2 = math.log(2.0)
SCALE = math.sqrt(5.0) / LN2
LINEAR = 3.0 / LN2
CONST = 3.0 / (LN2 * LN2)
OUTER = LN2 * LN2 / 3.0
TINY = 1e-30

BLOCK = 1024
NEAR = 8
REPS = 8
DY = (0, 1, -1, 2, -2, 3, -3, 4)


def place():
    b = lax.axis_index("blk")
    p = lax.axis_index("rep")
    return b // 8, (b // 4) % 2, b % 4, p // 2, p % 2


def device(y, zh, x, zl, c):
    return ((y * 2 + zh) * 4 + x, zl * 2 + c)


def partner(k, sign):
    y, zh, x, zl, c = place()
    outer = 1 - ((zl + 1) // 2) % 2
    other_zl = zl + outer * (3 - 2 * zl)
    other_zh = zh + outer * (1 - 2 * zh)
    reader = zl if sign > 0 else other_zl
    dx = (reader // 2 * 2 + c + k) % 4
    return device((y + sign * DY[k] + 8) % 8, other_zh, (x + sign * dx + 4) % 4, other_zl, c)


def rep_peer(k):
    return (lax.axis_index("blk"), (lax.axis_index("rep") + k) % REPS)


def y_peer(k):
    y, zh, x, zl, c = place()
    return device((y + k) % 8, zh, x, zl, c)


def zx_peer(k):
    y, zh, x, zl, c = place()
    zh_move, dx = k // 4, k % 4
    if zh_move:
        return device(y, 1 - zh, (x + dx) % 4, 3 - zl, c)
    return device(y, zh, (x + dx) % 4, zl, c)


def parts3(value):
    a = value.astype(BF16).astype(F32)
    rest = value - a
    b = rest.astype(BF16).astype(F32)
    c = (rest - b).astype(BF16).astype(F32)
    return a, b, c


PAIRS = ((0, 0), (0, 1), (0, 2), (1, 0), (1, 1), (2, 0))


def augmented(places, own):
    row = lax.broadcasted_iota(jnp.int32, (8, places.shape[1]), 0)
    parts = parts3(jnp.where(row < 4, places, 0.0))
    groups = []
    for a, b in PAIRS:
        if own:
            part = parts[b]
            length = jnp.broadcast_to(part[3:4], part.shape)
            group = jnp.where(row < 3, part, 0.0)
            group = jnp.where(row == 3, 1.0 if b == 0 else 0.0, group)
            group = jnp.where(row == 4, length if a == 0 else 0.0, group)
        else:
            part = parts[a]
            group = jnp.where(row < 3, -2.0 * part, jnp.where(row == 3, part if b == 0 else 0.0, 0.0))
            group = jnp.where(row == 4, 1.0 if a == 0 else 0.0, group)
        groups.append(group)
    groups.append(jnp.zeros((128 - 8 * len(PAIRS), places.shape[1]), F32))
    return jnp.concatenate(groups, axis=0)


def two_terms(vector):
    lead = vector.astype(BF16).astype(F32)
    return jnp.concatenate([lead, vector - lead, jnp.zeros((8, vector.shape[1]), F32)], axis=0).astype(BF16)


def matmul(a, b):
    return jnp.dot(a, b, preferred_element_type=F32)


def kernel(coords, noise, right, x_out, res_out, packet, packets, high, low, own_aug, part1, image1, images, part2,
           sums, sums_y, sums_zx, send, recv):
    y, zh, x, zl, c = place()
    rep = lax.axis_index("rep")
    own_first = jnp.logical_and(zl == 1, c == 0)

    def copy(src, dst, index, to):
        return pltpu.make_async_remote_copy(
            src_ref=src, dst_ref=dst, send_sem=send.at[index], recv_sem=recv.at[index], device_id=to,
            device_id_type=MESH,
        )

    barrier = pltpu.get_barrier_semaphore()
    for k in range(1, REPS):
        pl.semaphore_signal(barrier, inc=1, device_id=rep_peer(k), device_id_type=MESH)
    for k in range(1, NEAR):
        pl.semaphore_signal(barrier, inc=1, device_id=partner(k, 1), device_id_type=MESH)

    @pl.when(jnp.logical_not(own_first))
    def _():
        pl.semaphore_signal(barrier, inc=1, device_id=partner(0, 1), device_id_type=MESH)

    along = lax.broadcasted_iota(jnp.int32, (3, BLOCK), 0)
    centred = (coords[...] - jnp.where(along == 0, 6.0, 2.0)) * SCALE
    packet[0:3] = centred
    packet[3:4] = jnp.sum(centred * centred, axis=0, keepdims=True)
    packet[4:8] = right[...]
    own_aug[...] = augmented(packet[...], True).astype(BF16)

    @pl.when(own_first)
    def _():
        pl.semaphore_wait(barrier, NEAR + REPS - 2)
        packets[0] = packet[...]

    @pl.when(jnp.logical_not(own_first))
    def _():
        pl.semaphore_wait(barrier, NEAR + REPS - 1)
        copy(packet, packets.at[0], 0, partner(0, -1)).start()

    for k in range(1, NEAR):
        copy(packet, packets.at[k], k, partner(k, -1)).start()

    def wait_near(buffers, k, base):
        @pl.when(jnp.logical_not(jnp.logical_and(own_first, k == 0)))
        def _():
            copy(buffers.at[k], buffers.at[k], base + k, rep_peer(1)).wait_recv()

    def build(k, total):
        wait_near(packets, k, 0)
        block = packets[k]
        remote = augmented(block, False).T.astype(BF16)
        dist = jnp.maximum(matmul(remote, own_aug[...]), TINY)
        t = dist * lax.rsqrt(dist)
        value = ((t + LINEAR) * t + CONST) * jnp.exp2(-t)
        lead = value.astype(BF16)
        rest = (value - lead.astype(F32)).astype(BF16)
        rows = pl.ds(pl.multiple_of(k * BLOCK, BLOCK), BLOCK)
        high[rows, :] = lead
        low[rows, :] = rest
        vector = two_terms(block[4:8] * OUTER)
        return total + matmul(vector, lead) + matmul(vector, rest)

    def again(k, total):
        wait_near(images, k, NEAR + REPS)
        rows = pl.ds(pl.multiple_of(k * BLOCK, BLOCK), BLOCK)
        vector = two_terms(images[k] * OUTER)
        return total + matmul(vector, high[rows, :]) + matmul(vector, low[rows, :])

    def over_reps(part, total, base):
        part[rep] = total[0:4] + total[4:8]
        for k in range(1, REPS):
            copy(part.at[rep], part.at[rep], base + k, rep_peer(k)).start()
        for k in range(1, REPS):
            copy(part.at[rep], part.at[rep], base + k, rep_peer(k)).wait_recv()
        whole = part[0]
        for q in range(1, REPS):
            whole = whole + part[q]
        return whole

    zeros = jnp.zeros((16, BLOCK), F32)
    r0 = right[...]
    total = lax.fori_loop(0, NEAR, build, zeros)
    w1 = over_reps(part1, total, NEAR) + noise[...] * r0
    image1[...] = w1

    base = NEAR + REPS
    for k in range(1, NEAR):
        copy(image1, images.at[k], base + k, partner(k, -1)).start()

    @pl.when(own_first)
    def _():
        images[0] = image1[...]

    @pl.when(jnp.logical_not(own_first))
    def _():
        copy(image1, images.at[0], base, partner(0, -1)).start()

    total = lax.fori_loop(0, NEAR, again, zeros)
    w1 = image1[...]
    w2 = over_reps(part2, total, base + NEAR) + noise[...] * w1

    lane = lax.broadcasted_iota(jnp.int32, (4, 128), 1)
    grams = jnp.zeros((4, 128), F32)
    for at, (left, other) in enumerate(((r0, r0), (r0, w1), (w1, w1), (r0, w2), (w1, w2))):
        grams = jnp.where(lane == at, jnp.sum(left * other, axis=1, keepdims=True), grams)
    base = base + NEAR + REPS
    b = lax.axis_index("blk")

    sums_y[y] = grams
    for k in range(1, 8):
        copy(sums_y.at[y], sums_y.at[y], base + k, y_peer(k)).start()
    for k in range(1, 8):
        copy(sums_y.at[y], sums_y.at[y], base + k, y_peer(k)).wait_recv()
    grams = sums_y[0]
    for q in range(1, 8):
        grams = grams + sums_y[q]

    base = base + 8
    mine = b % 8
    sums_zx[mine] = grams
    for k in range(1, 8):
        copy(sums_zx.at[mine], sums_zx.at[mine], base + k, zx_peer(k)).start()
    for k in range(1, 8):
        copy(sums_zx.at[mine], sums_zx.at[mine], base + k, zx_peer(k)).wait_recv()
    grams = sums_zx[0]
    for q in range(1, 8):
        grams = grams + sums_zx[q]

    g00, g01, g11, g02, g12 = (grams[:, at:at + 1] for at in range(5))
    alpha = g00 / g01
    new = g00 - 2.0 * alpha * g01 + alpha * alpha * g11
    more = 1.0 + new / g00
    bottom = more * more * g01 - alpha * more * (g02 + g11) + alpha * alpha * g12
    alpha2 = new / bottom
    direction = more * r0 - alpha * w1
    image = more * w1 - alpha * w2
    x_out[...] = alpha * r0 + alpha2 * direction
    res_out[...] = (r0 - alpha * w1) - alpha2 * image

    for k in range(1, NEAR):
        copy(packet, packets.at[k], k, partner(k, -1)).wait_send()
        copy(image1, images.at[k], NEAR + REPS + k, partner(k, -1)).wait_send()

    @pl.when(jnp.logical_not(own_first))
    def _():
        copy(packet, packets.at[0], 0, partner(0, -1)).wait_send()
        copy(image1, images.at[0], NEAR + REPS, partner(0, -1)).wait_send()

    for k in range(1, REPS):
        copy(part1.at[rep], part1.at[rep], NEAR + k, rep_peer(k)).wait_send()
        copy(part2.at[rep], part2.at[rep], 2 * NEAR + REPS + k, rep_peer(k)).wait_send()
    for k in range(1, 8):
        copy(sums_y.at[y], sums_y.at[y], 2 * (NEAR + REPS) + k, y_peer(k)).wait_send()
        copy(sums_zx.at[mine], sums_zx.at[mine], 2 * (NEAR + REPS) + 8 + k, zx_peer(k)).wait_send()


def local(coords, noise, right_side):
    vmem = pl.BlockSpec(memory_space=pltpu.VMEM)
    field = jax.ShapeDtypeStruct((4, BLOCK), F32)
    copies = 2 * (NEAR + REPS) + 16
    call = pl.pallas_call(
        kernel,
        out_shape=(field, field),
        in_specs=[vmem] * 3,
        out_specs=(vmem, vmem),
        scratch_shapes=[
            pltpu.VMEM((8, BLOCK), F32),
            pltpu.VMEM((NEAR, 8, BLOCK), F32),
            pltpu.VMEM((NEAR * BLOCK, BLOCK), BF16),
            pltpu.VMEM((NEAR * BLOCK, BLOCK), BF16),
            pltpu.VMEM((128, BLOCK), BF16),
            pltpu.VMEM((REPS, 4, BLOCK), F32),
            pltpu.VMEM((4, BLOCK), F32),
            pltpu.VMEM((NEAR, 4, BLOCK), F32),
            pltpu.VMEM((REPS, 4, BLOCK), F32),
            pltpu.VMEM((4, 128), F32),
            pltpu.VMEM((8, 4, 128), F32),
            pltpu.VMEM((8, 4, 128), F32),
            pltpu.SemaphoreType.DMA((copies,)),
            pltpu.SemaphoreType.DMA((copies,)),
        ],
        compiler_params=pltpu.CompilerParams(
            collective_id=0, has_side_effects=True, vmem_limit_bytes=60 * 1024 * 1024
        ),
    )
    return call(coords, noise[None, :], right_side)


def solution(mesh):
    return jax.shard_map(
        local,
        mesh=mesh,
        in_specs=(P(None, "blk"), P("blk"), P(None, "blk")),
        out_specs=(P(None, "blk"), P(None, "blk")),
        check_vma=False,
    )
```

```python
import functools
import math

import jax
import jax.numpy as jnp
from jax import lax
from jax.experimental import pallas as pl
from jax.experimental.pallas import tpu as pltpu
from jax.sharding import PartitionSpec as P

F32 = jnp.float32
BF16 = jnp.bfloat16
MESH = pl.DeviceIdType.MESH

LN2 = math.log(2.0)
SCALE = math.sqrt(5.0) / LN2
LINEAR = 3.0 / LN2
CONST = 3.0 / (LN2 * LN2)
OUTER = LN2 * LN2 / 3.0
TINY = 1e-30

BLOCK = 1024
NEAR = 8
WHOLE = 4
PARTS = 4
WIDTH = BLOCK // PARTS
REPS = 8
DY = (0, 1, -1, 2, -2, 3, -3, 4)


def place():
    b = lax.axis_index("blk")
    p = lax.axis_index("rep")
    return b // 8, (b // 4) % 2, b % 4, p // 2, p % 2


def device(y, zh, x, zl, c):
    return ((y * 2 + zh) * 4 + x, zl * 2 + c)


def partner(k, sign, relayed=False):
    y, zh, x, zl, c = place()
    outer = 0 if relayed else 1 - ((zl + 1) // 2) % 2
    other_zl = zl + outer * (3 - 2 * zl)
    other_zh = zh + outer * (1 - 2 * zh)
    reader = zl if sign > 0 else other_zl
    dx = (reader // 2 * 2 + c + k) % 4
    return device((y + sign * DY[k] + 8) % 8, other_zh, (x + sign * dx + 4) % 4, other_zl, c)


def over_border():
    y, zh, x, zl, c = place()
    return device(y, 1 - zh, x, 3 - zl, c)


def rep_peer(k):
    return (lax.axis_index("blk"), (lax.axis_index("rep") + k) % REPS)


def y_peer(k):
    y, zh, x, zl, c = place()
    return device((y + k) % 8, zh, x, zl, c)


def zx_peer(k):
    y, zh, x, zl, c = place()
    zh_move, dx = k // 4, k % 4
    if zh_move:
        return device(y, 1 - zh, (x + dx) % 4, 3 - zl, c)
    return device(y, zh, (x + dx) % 4, zl, c)


def parts3(value):
    a = value.astype(BF16).astype(F32)
    rest = value - a
    b = rest.astype(BF16).astype(F32)
    c = (rest - b).astype(BF16).astype(F32)
    return a, b, c


PAIRS = ((0, 0), (0, 1), (0, 2), (1, 0), (1, 1), (2, 0))


def augmented(places, own):
    row = lax.broadcasted_iota(jnp.int32, (8, places.shape[1]), 0)
    parts = parts3(jnp.where(row < 4, places, 0.0))
    groups = []
    for a, b in PAIRS:
        if own:
            part = parts[b]
            length = jnp.broadcast_to(part[3:4], part.shape)
            group = jnp.where(row < 3, part, 0.0)
            group = jnp.where(row == 3, 1.0 if b == 0 else 0.0, group)
            group = jnp.where(row == 4, length if a == 0 else 0.0, group)
        else:
            part = parts[a]
            group = jnp.where(row < 3, -2.0 * part, jnp.where(row == 3, part if b == 0 else 0.0, 0.0))
            group = jnp.where(row == 4, 1.0 if a == 0 else 0.0, group)
        groups.append(group)
    groups.append(jnp.zeros((128 - 8 * len(PAIRS), places.shape[1]), F32))
    return jnp.concatenate(groups, axis=0)


def two_terms(vector):
    lead = vector.astype(BF16).astype(F32)
    return jnp.concatenate([lead, vector - lead, jnp.zeros((8, vector.shape[1]), F32)], axis=0).astype(BF16)


def matmul(a, b):
    return jnp.dot(a, b, preferred_element_type=F32)


def kernel(coords_in, noise_in, right_in, out, packet, origin, packets, high, low, own_aug, remote_aug, partial, part1,
           image1, images, part2, sums_rep, sums_y, sums_zx, send_near, recv_near, send1, recv1, send_image, recv_image,
           send_end, recv_end, coords, noise, right, load):
    y, zh, x, zl, c = place()
    rep = lax.axis_index("rep")
    own_first = jnp.logical_and(zl == 1, c == 0)
    not_own = jnp.logical_not(own_first)
    outer = 1 - ((zl + 1) // 2) % 2
    group_first = zl // 2 * 2 + c == 0
    not_group = jnp.logical_not(group_first)

    def copy(src, dst, sent, received, to):
        return pltpu.make_async_remote_copy(
            src_ref=src, dst_ref=dst, send_sem=sent, recv_sem=received, device_id=to, device_id_type=MESH
        )

    barrier = pltpu.get_barrier_semaphore()
    @pl.when(outer == 1)
    def _():
        pl.semaphore_signal(barrier, inc=1, device_id=over_border(), device_id_type=MESH)

    for k in range(1, NEAR):
        pl.semaphore_signal(barrier, inc=1, device_id=partner(k, 1, True), device_id_type=MESH)

    @pl.when(not_group)
    def _():
        pl.semaphore_signal(barrier, inc=1, device_id=partner(0, 1, True), device_id_type=MESH)

    for k in range(1, REPS):
        pl.semaphore_signal(barrier, inc=1, device_id=rep_peer(k), device_id_type=MESH)

    loads = [
        pltpu.make_async_copy(given, held_here, load.at[at])
        for at, (given, held_here) in enumerate(((coords_in, coords), (right_in, right), (noise_in, noise)))
    ]
    for one in loads:
        one.start()
    for one in loads:
        one.wait()
    along = lax.broadcasted_iota(jnp.int32, (3, BLOCK), 0)
    centred = (coords[...] - jnp.where(along == 0, 6.0, 2.0)) * SCALE
    packet[0:3] = centred
    packet[3:4] = jnp.sum(centred * centred, axis=0, keepdims=True)
    packet[4:8] = right[...]

    def near_copy(k):
        return copy(origin, packets.at[k], send_near.at[k], recv_near.at[k], partner(k, -1, True))

    def image_copy(q, k):
        return copy(image1.at[q], images.at[q, k], send_image.at[q, k], recv_image.at[q, k], partner(k, -1))

    def part_copy(q, k):
        return copy(part1.at[q, rep], part1.at[q, rep], send1.at[q, k], recv1.at[q, k], rep_peer(k))

    def crossing():
        return copy(packet, origin, send_near.at[NEAR], recv_near.at[NEAR], over_border())

    signals = NEAR + REPS - 1

    @pl.when(jnp.logical_and(outer == 0, group_first))
    def _():
        pl.semaphore_wait(barrier, signals - 1)

    @pl.when(jnp.logical_and(outer == 0, not_group))
    def _():
        pl.semaphore_wait(barrier, signals)

    @pl.when(jnp.logical_and(outer == 1, group_first))
    def _():
        pl.semaphore_wait(barrier, signals)

    @pl.when(jnp.logical_and(outer == 1, not_group))
    def _():
        pl.semaphore_wait(barrier, signals + 1)

    @pl.when(outer == 1)
    def _():
        crossing().start()

    own_aug[...] = augmented(packet[...], True).astype(BF16)

    @pl.when(outer == 1)
    def _():
        crossing().wait_recv()

    @pl.when(outer == 0)
    def _():
        origin[...] = packet[...]

    @pl.when(group_first)
    def _():
        packets[0] = origin[...]

    @pl.when(not_group)
    def _():
        near_copy(0).start()

    for k in range(1, NEAR):
        near_copy(k).start()


    def rows(k):
        return pl.ds(pl.multiple_of(k * BLOCK, BLOCK), BLOCK)

    def held(k, q):
        return pl.ds(pl.multiple_of((q * NEAR + k) * WIDTH, WIDTH), WIDTH)

    def fetch(k):
        @pl.when(jnp.logical_not(jnp.logical_and(group_first, k == 0)))
        def _():
            copy(packets.at[k], packets.at[k], send_near.at[k], recv_near.at[k], rep_peer(1)).wait_recv()

        remote_aug[rows(k), :] = augmented(packets[k], False).astype(BF16).T

    def values(dist):
        dist = jnp.maximum(dist, TINY)
        t = dist * lax.rsqrt(dist)
        value = ((t + LINEAR) * t + CONST) * jnp.exp2(-t)
        lead = value.astype(BF16)
        return lead, (value - lead.astype(F32)).astype(BF16)

    def build_whole(k, total):
        vector = two_terms(packets[k, 4:8] * OUTER)
        lead, rest = values(matmul(remote_aug[rows(k), :], own_aug[...]))
        for q in range(PARTS):
            high[held(k, q), :] = lead[q * WIDTH:(q + 1) * WIDTH]
            low[held(k, q), :] = rest[q * WIDTH:(q + 1) * WIDTH]
        fetch(k + 1)
        return total + matmul(vector, lead) + matmul(vector, rest)

    zeros = jnp.zeros((16, BLOCK), F32)
    fetch(0)
    partial[...] = lax.fori_loop(0, WHOLE, build_whole, zeros)
    for k in range(WHOLE + 1, NEAR):
        fetch(k)

    def image_part(q):
        for k in range(1, REPS):
            part_copy(q, k).wait_recv()
        whole = part1[q, 0]
        for other in range(1, REPS):
            whole = whole + part1[q, other]
        cols = pl.ds(pl.multiple_of(q * WIDTH, WIDTH), WIDTH)
        image1[q] = whole + noise[:, cols] * right[:, cols]

        @pl.when(own_first)
        def _():
            images[q, 0] = image1[q]

        @pl.when(not_own)
        def _():
            image_copy(q, 0).start()

        for k in range(1, NEAR):
            image_copy(q, k).start()

    def build_part(q, _):
        cols = pl.ds(pl.multiple_of(q * WIDTH, WIDTH), WIDTH)
        total = partial[:, cols]
        own = own_aug[:, cols]
        for k in range(WHOLE, NEAR):
            vector = two_terms(packets[k, 4:8] * OUTER)
            lead, rest = values(matmul(remote_aug[rows(k), :], own))
            for part in range(PARTS):
                high[held(k, part), cols] = lead[part * WIDTH:(part + 1) * WIDTH]
                low[held(k, part), cols] = rest[part * WIDTH:(part + 1) * WIDTH]
            total = total + matmul(vector, lead) + matmul(vector, rest)
        part1[q, rep] = total[0:4] + total[4:8]
        for k in range(1, REPS):
            part_copy(q, k).start()

        @pl.when(q >= 2)
        def _():
            image_part(q - 2)

        return 0

    lax.fori_loop(0, PARTS, build_part, 0)
    image_part(PARTS - 2)
    image_part(PARTS - 1)

    def again(n, total):
        q, first = n // 2, n % 2 * 4

        @pl.when(jnp.logical_not(jnp.logical_and(own_first, first == 0)))
        def _():
            arrived(q, first)

        for k in range(1, 4):
            arrived(q, first + k)
        vector = two_terms(jnp.concatenate([images[q, first + k] for k in range(4)], axis=1) * OUTER)
        part = rows(n)
        return total + matmul(vector, high[part, :]) + matmul(vector, low[part, :])

    def arrived(q, k):
        copy(images.at[q, k], images.at[q, k], send_image.at[q, k], recv_image.at[q, k], rep_peer(1)).wait_recv()

    total = lax.fori_loop(0, 2 * PARTS, again, zeros)
    own_part = total[0:4] + total[4:8]
    r0 = right[...]
    w1 = jnp.concatenate([image1[q] for q in range(PARTS)], axis=1)
    spread = noise[...] * w1

    lane = lax.broadcasted_iota(jnp.int32, (4, 128), 1)
    once = jnp.where(rep == 0, 1.0, 0.0)
    mine = own_part + once * spread
    grams = jnp.zeros((4, 128), F32)
    for at, product in enumerate((once * r0 * r0, once * r0 * w1, once * w1 * w1, r0 * mine, w1 * mine)):
        grams = jnp.where(lane == at, jnp.sum(product, axis=1, keepdims=True), grams)

    def over(slots, me, stage, peer, value):
        slots[me] = value
        copies = [
            copy(slots.at[me], slots.at[me], send_end.at[stage, k], recv_end.at[stage, k], peer(k)) for k in range(1, 8)
        ]
        for one in copies:
            one.start()
        return copies

    def added(slots, copies):
        for one in copies:
            one.wait_recv()
        value = slots[0]
        for other in range(1, 8):
            value = value + slots[other]
        return value

    across = lax.axis_index("blk") % 8
    first = over(sums_rep, rep, 0, rep_peer, grams)
    bulk = over(part2, rep, 3, rep_peer, own_part)
    second = over(sums_y, y, 1, y_peer, added(sums_rep, first))
    third = over(sums_zx, across, 2, zx_peer, added(sums_y, second))
    w2 = added(part2, bulk) + spread
    grams = added(sums_zx, third)

    g00, g01, g11, g02, g12 = (grams[:, at:at + 1] for at in range(5))
    alpha = g00 / g01
    new = g00 - 2.0 * alpha * g01 + alpha * alpha * g11
    more = 1.0 + new / g00
    bottom = more * more * g01 - alpha * more * (g02 + g11) + alpha * alpha * g12
    alpha2 = new / bottom
    direction = more * r0 - alpha * w1
    image = more * w1 - alpha * w2
    out[0:4] = alpha * r0 + alpha2 * direction
    out[4:8] = (r0 - alpha * w1) - alpha2 * image

    @pl.when(outer == 1)
    def _():
        crossing().wait_send()

    @pl.when(not_group)
    def _():
        near_copy(0).wait_send()

    for k in range(1, NEAR):
        near_copy(k).wait_send()
    for one in first + second + third + bulk:
        one.wait_send()

    def left(q, _):
        @pl.when(not_own)
        def _():
            image_copy(q, 0).wait_send()

        for k in range(1, NEAR):
            image_copy(q, k).wait_send()
        for k in range(1, REPS):
            part_copy(q, k).wait_send()
        return 0

    lax.fori_loop(0, PARTS, left, 0)


def local(coords, noise, right_side):
    vmem = pl.BlockSpec(memory_space=pltpu.VMEM)
    field = jax.ShapeDtypeStruct((8, BLOCK), F32)
    call = pl.pallas_call(
        kernel,
        out_shape=field,
        in_specs=[pl.BlockSpec(memory_space=pl.ANY)] * 3,
        out_specs=vmem,
        scratch_shapes=[
            pltpu.VMEM((8, BLOCK), F32),
            pltpu.VMEM((8, BLOCK), F32),
            pltpu.VMEM((NEAR, 8, BLOCK), F32),
            pltpu.VMEM((NEAR * BLOCK, BLOCK), BF16),
            pltpu.VMEM((NEAR * BLOCK, BLOCK), BF16),
            pltpu.VMEM((128, BLOCK), BF16),
            pltpu.VMEM((NEAR * BLOCK, 128), BF16),
            pltpu.VMEM((16, BLOCK), F32),
            pltpu.VMEM((PARTS, REPS, 4, WIDTH), F32),
            pltpu.VMEM((PARTS, 4, WIDTH), F32),
            pltpu.VMEM((PARTS, NEAR, 4, WIDTH), F32),
            pltpu.VMEM((REPS, 4, BLOCK), F32),
            pltpu.VMEM((REPS, 4, 128), F32),
            pltpu.VMEM((8, 4, 128), F32),
            pltpu.VMEM((8, 4, 128), F32),
            pltpu.SemaphoreType.DMA((NEAR + 1,)),
            pltpu.SemaphoreType.DMA((NEAR + 1,)),
            pltpu.SemaphoreType.DMA((PARTS, REPS)),
            pltpu.SemaphoreType.DMA((PARTS, REPS)),
            pltpu.SemaphoreType.DMA((PARTS, NEAR)),
            pltpu.SemaphoreType.DMA((PARTS, NEAR)),
            pltpu.SemaphoreType.DMA((4, 8)),
            pltpu.SemaphoreType.DMA((4, 8)),
            pltpu.VMEM((3, BLOCK), F32),
            pltpu.VMEM((1, BLOCK), F32),
            pltpu.VMEM((4, BLOCK), F32),
            pltpu.SemaphoreType.DMA((3,)),
        ],
        compiler_params=pltpu.CompilerParams(
            collective_id=0, has_side_effects=True, vmem_limit_bytes=60 * 1024 * 1024
        ),
    )
    both = call(coords, noise[None, :], right_side)
    return both[0:4], both[4:8]


def solution(mesh):
    return jax.shard_map(
        local,
        mesh=mesh,
        in_specs=(P(None, "blk"), P("blk"), P(None, "blk")),
        out_specs=(P(None, "blk"), P(None, "blk")),
        check_vma=False,
    )
```

```python
import functools
import math

import jax
import jax.numpy as jnp
from jax import lax
from jax.experimental import pallas as pl
from jax.experimental.pallas import tpu as pltpu
from jax.sharding import PartitionSpec as P

F32 = jnp.float32
BF16 = jnp.bfloat16
MESH = pl.DeviceIdType.MESH

LN2 = math.log(2.0)
SCALE = math.sqrt(5.0) / LN2
LINEAR = 3.0 / LN2
CONST = 3.0 / (LN2 * LN2)
OUTER = LN2 * LN2 / 3.0
TINY = 1e-30

BLOCK = 1024
NEAR = 8
WHOLE = 6
PARTS = 4
WIDTH = BLOCK // PARTS
REPS = 8
DY = (0, 1, -1, 2, -2, 3, -3, 4)


def place():
    b = lax.axis_index("blk")
    p = lax.axis_index("rep")
    return b // 8, (b // 4) % 2, b % 4, p // 2, p % 2


def device(y, zh, x, zl, c):
    return ((y * 2 + zh) * 4 + x, zl * 2 + c)


def partner(k, sign):
    y, zh, x, zl, c = place()
    outer = 1 - ((zl + 1) // 2) % 2
    other_zl = zl + outer * (3 - 2 * zl)
    other_zh = zh + outer * (1 - 2 * zh)
    reader = zl if sign > 0 else other_zl
    dx = (reader // 2 * 2 + c) % 4
    return device((y + sign * DY[k] + 8) % 8, other_zh, (x + sign * dx + 4) % 4, other_zl, c)


def y_neighbour(step):
    y, zh, x, zl, c = place()
    return device((y + step + 8) % 8, zh, x, zl, c)


def rep_peer(k):
    return (lax.axis_index("blk"), (lax.axis_index("rep") + k) % REPS)


def y_peer(k):
    y, zh, x, zl, c = place()
    return device((y + k) % 8, zh, x, zl, c)


def zx_peer(k):
    y, zh, x, zl, c = place()
    zh_move, dx = k // 4, k % 4
    if zh_move:
        return device(y, 1 - zh, (x + dx) % 4, 3 - zl, c)
    return device(y, zh, (x + dx) % 4, zl, c)


def parts3(value):
    a = value.astype(BF16).astype(F32)
    rest = value - a
    b = rest.astype(BF16).astype(F32)
    c = (rest - b).astype(BF16).astype(F32)
    return a, b, c


PAIRS = ((0, 0), (0, 1), (0, 2), (1, 0), (1, 1), (2, 0))


def augmented(places, own):
    row = lax.broadcasted_iota(jnp.int32, (8, places.shape[1]), 0)
    parts = parts3(jnp.where(row < 4, places, 0.0))
    groups = []
    for a, b in PAIRS:
        if own:
            part = parts[b]
            length = jnp.broadcast_to(part[3:4], part.shape)
            group = jnp.where(row < 3, part, 0.0)
            group = jnp.where(row == 3, 1.0 if b == 0 else 0.0, group)
            group = jnp.where(row == 4, length if a == 0 else 0.0, group)
        else:
            part = parts[a]
            group = jnp.where(row < 3, -2.0 * part, jnp.where(row == 3, part if b == 0 else 0.0, 0.0))
            group = jnp.where(row == 4, 1.0 if a == 0 else 0.0, group)
        groups.append(group)
    groups.append(jnp.zeros((128 - 8 * len(PAIRS), places.shape[1]), F32))
    return jnp.concatenate(groups, axis=0)


def two_terms(vector):
    lead = vector.astype(BF16).astype(F32)
    return jnp.concatenate([lead, vector - lead, jnp.zeros((8, vector.shape[1]), F32)], axis=0).astype(BF16)


def matmul(a, b):
    return jnp.dot(a, b, preferred_element_type=F32)


def kernel(coords_in, noise_in, right_in, out, packet, packets, high, low, own_aug, remote_aug, partial, part1,
           image1, images, part2, sums_rep, sums_y, sums_zx, send_near, recv_near, send1, recv1, send_image, recv_image,
           send_end, recv_end, coords, noise, right, load):
    y, zh, x, zl, c = place()
    rep = lax.axis_index("rep")
    own_first = jnp.logical_and(zl == 1, c == 0)
    not_own = jnp.logical_not(own_first)

    def copy(src, dst, sent, received, to):
        return pltpu.make_async_remote_copy(
            src_ref=src, dst_ref=dst, send_sem=sent, recv_sem=received, device_id=to, device_id_type=MESH
        )

    barrier = pltpu.get_barrier_semaphore()
    for step in (1, -1):
        pl.semaphore_signal(barrier, inc=1, device_id=y_neighbour(step), device_id_type=MESH)

    @pl.when(not_own)
    def _():
        pl.semaphore_signal(barrier, inc=1, device_id=partner(0, 1), device_id_type=MESH)

    for k in range(1, REPS):
        pl.semaphore_signal(barrier, inc=1, device_id=rep_peer(k), device_id_type=MESH)

    loads = [
        pltpu.make_async_copy(given, held_here, load.at[at])
        for at, (given, held_here) in enumerate(((coords_in, coords), (right_in, right), (noise_in, noise)))
    ]
    for one in loads:
        one.start()
    for one in loads:
        one.wait()
    along = lax.broadcasted_iota(jnp.int32, (3, BLOCK), 0)
    centred = (coords[...] - jnp.where(along == 0, 6.0, 2.0)) * SCALE
    packet[0:3] = centred
    packet[3:4] = jnp.sum(centred * centred, axis=0, keepdims=True)
    packet[4:8] = right[...]

    def first_copy():
        return copy(packet, packets.at[0], send_near.at[0], recv_near.at[0], partner(0, -1))

    def turn_copy():
        return copy(packets.at[0], packets.at[1], send_near.at[1], recv_near.at[1], y_neighbour(-1))

    def ring_copy(k):
        return copy(
            packets.at[k], packets.at[k + 2], send_near.at[k + 2], recv_near.at[k + 2], y_neighbour(1 - 2 * (k % 2))
        )

    def image_copy(q, k):
        return copy(image1.at[q], images.at[q, k], send_image.at[q, k], recv_image.at[q, k], partner(k, -1))

    def part_copy(q, k):
        return copy(part1.at[q, rep], part1.at[q, rep], send1.at[q, k], recv1.at[q, k], rep_peer(k))

    @pl.when(own_first)
    def _():
        pl.semaphore_wait(barrier, REPS + 1)
        packets[0] = packet[...]

    @pl.when(not_own)
    def _():
        pl.semaphore_wait(barrier, REPS + 2)
        first_copy().start()

    own_aug[...] = augmented(packet[...], True).astype(BF16)

    def rows(k):
        return pl.ds(pl.multiple_of(k * BLOCK, BLOCK), BLOCK)

    def held(k, q):
        return pl.ds(pl.multiple_of((q * NEAR + k) * WIDTH, WIDTH), WIDTH)

    def fetch(k):
        @pl.when(jnp.logical_not(jnp.logical_and(own_first, k == 0)))
        def _():
            copy(packets.at[k], packets.at[k], send_near.at[k], recv_near.at[k], rep_peer(1)).wait_recv()

        @pl.when(k < NEAR - 2)
        def _():
            ring_copy(k).start()

        @pl.when(k == 0)
        def _():
            turn_copy().start()

        remote_aug[rows(k), :] = augmented(packets[k], False).astype(BF16).T

    def values(dist):
        dist = jnp.maximum(dist, TINY)
        t = dist * lax.rsqrt(dist)
        value = ((t + LINEAR) * t + CONST) * jnp.exp2(-t)
        lead = value.astype(BF16)
        return lead, (value - lead.astype(F32)).astype(BF16)

    def build_whole(k, total):
        vector = two_terms(packets[k, 4:8] * OUTER)
        lead, rest = values(matmul(remote_aug[rows(k), :], own_aug[...]))
        for q in range(PARTS):
            high[held(k, q), :] = lead[q * WIDTH:(q + 1) * WIDTH]
            low[held(k, q), :] = rest[q * WIDTH:(q + 1) * WIDTH]
        fetch(k + 1)
        return total + matmul(vector, lead) + matmul(vector, rest)

    zeros = jnp.zeros((16, BLOCK), F32)
    fetch(jnp.int32(0))
    partial[...] = lax.fori_loop(0, WHOLE, build_whole, zeros)
    for k in range(WHOLE + 1, NEAR):
        fetch(jnp.int32(k))

    def image_part(q):
        for k in range(1, REPS):
            part_copy(q, k).wait_recv()
        whole = part1[q, 0]
        for other in range(1, REPS):
            whole = whole + part1[q, other]
        cols = pl.ds(pl.multiple_of(q * WIDTH, WIDTH), WIDTH)
        image1[q] = whole + noise[:, cols] * right[:, cols]

        for k in range(NEAR - 1, 0, -1):
            image_copy(q, k).start()

        @pl.when(own_first)
        def _():
            images[q, 0] = image1[q]

        @pl.when(not_own)
        def _():
            image_copy(q, 0).start()

    def build_part(q, _):
        cols = pl.ds(pl.multiple_of(q * WIDTH, WIDTH), WIDTH)
        total = partial[:, cols]
        own = own_aug[:, cols]
        for k in range(WHOLE, NEAR):
            vector = two_terms(packets[k, 4:8] * OUTER)
            lead, rest = values(matmul(remote_aug[rows(k), :], own))
            for part in range(PARTS):
                high[held(k, part), cols] = lead[part * WIDTH:(part + 1) * WIDTH]
                low[held(k, part), cols] = rest[part * WIDTH:(part + 1) * WIDTH]
            total = total + matmul(vector, lead) + matmul(vector, rest)
        part1[q, rep] = total[0:4] + total[4:8]
        for k in range(1, REPS):
            part_copy(q, k).start()

        return 0

    lax.fori_loop(0, PARTS, build_part, 0)
    for q in range(PARTS):
        image_part(q)

    def again(n, total):
        q, first = n // 2, n % 2 * 4

        @pl.when(jnp.logical_not(jnp.logical_and(own_first, first == 0)))
        def _():
            arrived(q, first)

        for k in range(1, 4):
            arrived(q, first + k)
        vector = two_terms(jnp.concatenate([images[q, first + k] for k in range(4)], axis=1) * OUTER)
        part = rows(n)
        return total + matmul(vector, high[part, :]) + matmul(vector, low[part, :])

    def arrived(q, k):
        copy(images.at[q, k], images.at[q, k], send_image.at[q, k], recv_image.at[q, k], rep_peer(1)).wait_recv()

    total = lax.fori_loop(0, 2 * PARTS, again, zeros)
    own_part = total[0:4] + total[4:8]
    r0 = right[...]
    w1 = jnp.concatenate([image1[q] for q in range(PARTS)], axis=1)
    spread = noise[...] * w1

    lane = lax.broadcasted_iota(jnp.int32, (4, 128), 1)
    once = jnp.where(rep == 0, 1.0, 0.0)
    mine = own_part + once * spread
    grams = jnp.zeros((4, 128), F32)
    for at, product in enumerate((once * r0 * r0, once * r0 * w1, once * w1 * w1, r0 * mine, w1 * mine)):
        grams = jnp.where(lane == at, jnp.sum(product, axis=1, keepdims=True), grams)

    def over(slots, me, stage, peer, value):
        slots[me] = value
        copies = [
            copy(slots.at[me], slots.at[me], send_end.at[stage, k], recv_end.at[stage, k], peer(k)) for k in range(1, 8)
        ]
        for one in copies:
            one.start()
        return copies

    def added(slots, copies):
        for one in copies:
            one.wait_recv()
        value = slots[0]
        for other in range(1, 8):
            value = value + slots[other]
        return value

    across = lax.axis_index("blk") % 8
    first = over(sums_rep, rep, 0, rep_peer, grams)
    bulk = over(part2, rep, 3, rep_peer, own_part)
    second = over(sums_y, y, 1, y_peer, added(sums_rep, first))
    third = over(sums_zx, across, 2, zx_peer, added(sums_y, second))
    w2 = added(part2, bulk) + spread
    grams = added(sums_zx, third)

    g00, g01, g11, g02, g12 = (grams[:, at:at + 1] for at in range(5))
    alpha = g00 / g01
    new = g00 - 2.0 * alpha * g01 + alpha * alpha * g11
    more = 1.0 + new / g00
    bottom = more * more * g01 - alpha * more * (g02 + g11) + alpha * alpha * g12
    alpha2 = new / bottom
    direction = more * r0 - alpha * w1
    image = more * w1 - alpha * w2
    out[0:4] = alpha * r0 + alpha2 * direction
    out[4:8] = (r0 - alpha * w1) - alpha2 * image

    @pl.when(not_own)
    def _():
        first_copy().wait_send()

    turn_copy().wait_send()
    for k in range(NEAR - 2):
        ring_copy(k).wait_send()
    for one in first + second + third + bulk:
        one.wait_send()

    def left(q, _):
        @pl.when(not_own)
        def _():
            image_copy(q, 0).wait_send()

        for k in range(1, NEAR):
            image_copy(q, k).wait_send()
        for k in range(1, REPS):
            part_copy(q, k).wait_send()
        return 0

    lax.fori_loop(0, PARTS, left, 0)


def local(coords, noise, right_side):
    vmem = pl.BlockSpec(memory_space=pltpu.VMEM)
    field = jax.ShapeDtypeStruct((8, BLOCK), F32)
    call = pl.pallas_call(
        kernel,
        out_shape=field,
        in_specs=[pl.BlockSpec(memory_space=pl.ANY)] * 3,
        out_specs=vmem,
        scratch_shapes=[
            pltpu.VMEM((8, BLOCK), F32),
            pltpu.VMEM((NEAR, 8, BLOCK), F32),
            pltpu.VMEM((NEAR * BLOCK, BLOCK), BF16),
            pltpu.VMEM((NEAR * BLOCK, BLOCK), BF16),
            pltpu.VMEM((128, BLOCK), BF16),
            pltpu.VMEM((NEAR * BLOCK, 128), BF16),
            pltpu.VMEM((16, BLOCK), F32),
            pltpu.VMEM((PARTS, REPS, 4, WIDTH), F32),
            pltpu.VMEM((PARTS, 4, WIDTH), F32),
            pltpu.VMEM((PARTS, NEAR, 4, WIDTH), F32),
            pltpu.VMEM((REPS, 4, BLOCK), F32),
            pltpu.VMEM((REPS, 4, 128), F32),
            pltpu.VMEM((8, 4, 128), F32),
            pltpu.VMEM((8, 4, 128), F32),
            pltpu.SemaphoreType.DMA((NEAR,)),
            pltpu.SemaphoreType.DMA((NEAR,)),
            pltpu.SemaphoreType.DMA((PARTS, REPS)),
            pltpu.SemaphoreType.DMA((PARTS, REPS)),
            pltpu.SemaphoreType.DMA((PARTS, NEAR)),
            pltpu.SemaphoreType.DMA((PARTS, NEAR)),
            pltpu.SemaphoreType.DMA((4, 8)),
            pltpu.SemaphoreType.DMA((4, 8)),
            pltpu.VMEM((3, BLOCK), F32),
            pltpu.VMEM((1, BLOCK), F32),
            pltpu.VMEM((4, BLOCK), F32),
            pltpu.SemaphoreType.DMA((3,)),
        ],
        compiler_params=pltpu.CompilerParams(
            collective_id=0, has_side_effects=True, vmem_limit_bytes=60 * 1024 * 1024
        ),
    )
    both = call(coords, noise[None, :], right_side)
    return both[0:4], both[4:8]


def solution(mesh):
    return jax.shard_map(
        local,
        mesh=mesh,
        in_specs=(P(None, "blk"), P("blk"), P(None, "blk")),
        out_specs=(P(None, "blk"), P(None, "blk")),
        check_vma=False,
    )
```

```python
import functools
import math

import jax
import jax.numpy as jnp
from jax import lax
from jax.experimental import pallas as pl
from jax.experimental.pallas import tpu as pltpu
from jax.sharding import PartitionSpec as P

F32 = jnp.float32
BF16 = jnp.bfloat16
MESH = pl.DeviceIdType.MESH

LN2 = math.log(2.0)
SCALE = math.sqrt(5.0) / LN2
LINEAR = 3.0 / LN2
CONST = 3.0 / (LN2 * LN2)
OUTER = LN2 * LN2 / 3.0
TINY = 1e-30

BLOCK = 1024
NEAR = 8
WHOLE = 6
PARTS = 4
WIDTH = BLOCK // PARTS
REPS = 8
DY = (0, 1, -1, 2, -2, 3, -3, 4)


def place():
    b = lax.axis_index("blk")
    p = lax.axis_index("rep")
    return b // 8, (b // 4) % 2, b % 4, p // 2, p % 2


def device(y, zh, x, zl, c):
    return ((y * 2 + zh) * 4 + x, zl * 2 + c)


def partner(k, sign):
    y, zh, x, zl, c = place()
    outer = 1 - ((zl + 1) // 2) % 2
    other_zl = zl + outer * (3 - 2 * zl)
    other_zh = zh + outer * (1 - 2 * zh)
    reader = zl if sign > 0 else other_zl
    dx = (reader // 2 * 2 + c) % 4
    return device((y + sign * DY[k] + 8) % 8, other_zh, (x + sign * dx + 4) % 4, other_zl, c)


def y_neighbour(step):
    y, zh, x, zl, c = place()
    return device((y + step + 8) % 8, zh, x, zl, c)


def rep_peer(k):
    return (lax.axis_index("blk"), (lax.axis_index("rep") + k) % REPS)


def y_peer(k):
    y, zh, x, zl, c = place()
    return device((y + k) % 8, zh, x, zl, c)


def zx_peer(k):
    y, zh, x, zl, c = place()
    zh_move, dx = k // 4, k % 4
    if zh_move:
        return device(y, 1 - zh, (x + dx) % 4, 3 - zl, c)
    return device(y, zh, (x + dx) % 4, zl, c)


def parts3(value):
    a = value.astype(BF16).astype(F32)
    rest = value - a
    b = rest.astype(BF16).astype(F32)
    c = (rest - b).astype(BF16).astype(F32)
    return a, b, c


PAIRS = ((0, 0), (0, 1), (0, 2), (1, 0), (1, 1), (2, 0))


def augmented(places, own):
    row = lax.broadcasted_iota(jnp.int32, (8, places.shape[1]), 0)
    parts = parts3(jnp.where(row < 4, places, 0.0))
    groups = []
    for a, b in PAIRS:
        if own:
            part = parts[b]
            length = jnp.broadcast_to(part[3:4], part.shape)
            group = jnp.where(row < 3, part, 0.0)
            group = jnp.where(row == 3, 1.0 if b == 0 else 0.0, group)
            group = jnp.where(row == 4, length if a == 0 else 0.0, group)
        else:
            part = parts[a]
            group = jnp.where(row < 3, -2.0 * part, jnp.where(row == 3, part if b == 0 else 0.0, 0.0))
            group = jnp.where(row == 4, 1.0 if a == 0 else 0.0, group)
        groups.append(group)
    groups.append(jnp.zeros((128 - 8 * len(PAIRS), places.shape[1]), F32))
    return jnp.concatenate(groups, axis=0)


def two_terms(vector):
    lead = vector.astype(BF16).astype(F32)
    return jnp.concatenate([lead, vector - lead, jnp.zeros((8, vector.shape[1]), F32)], axis=0).astype(BF16)


def matmul(a, b):
    return jnp.dot(a, b, preferred_element_type=F32)


def kernel(coords_in, noise_in, right_in, out, packet, packets, high, low, own_aug, remote_aug, partial, part1,
           image1, images, part2, sums_rep, sums_y, sums_zx, send_near, recv_near, send1, recv1, send_image, recv_image,
           send_end, recv_end, coords, noise, right, load):
    y, zh, x, zl, c = place()
    rep = lax.axis_index("rep")
    own_first = jnp.logical_and(zl == 1, c == 0)
    not_own = jnp.logical_not(own_first)

    def copy(src, dst, sent, received, to):
        return pltpu.make_async_remote_copy(
            src_ref=src, dst_ref=dst, send_sem=sent, recv_sem=received, device_id=to, device_id_type=MESH
        )

    barrier = pltpu.get_barrier_semaphore()
    for step in (1, -1):
        pl.semaphore_signal(barrier, inc=1, device_id=y_neighbour(step), device_id_type=MESH)

    @pl.when(not_own)
    def _():
        pl.semaphore_signal(barrier, inc=1, device_id=partner(0, 1), device_id_type=MESH)

    for k in range(1, REPS):
        pl.semaphore_signal(barrier, inc=1, device_id=rep_peer(k), device_id_type=MESH)

    loads = [
        pltpu.make_async_copy(given, held_here, load.at[at])
        for at, (given, held_here) in enumerate(((coords_in, coords), (right_in, right), (noise_in, noise)))
    ]
    for one in loads:
        one.start()
    for one in loads:
        one.wait()
    along = lax.broadcasted_iota(jnp.int32, (3, BLOCK), 0)
    centred = (coords[...] - jnp.where(along == 0, 6.0, 2.0)) * SCALE
    packet[0:3] = centred
    packet[3:4] = jnp.sum(centred * centred, axis=0, keepdims=True)
    packet[4:8] = right[...]

    def first_copy():
        return copy(packet, packets.at[0], send_near.at[0], recv_near.at[0], partner(0, -1))

    def turn_copy():
        return copy(packets.at[0], packets.at[1], send_near.at[1], recv_near.at[1], y_neighbour(-1))

    def ring_copy(k):
        return copy(
            packets.at[k], packets.at[k + 2], send_near.at[k + 2], recv_near.at[k + 2], y_neighbour(1 - 2 * (k % 2))
        )

    def image_copy(q, k):
        return copy(image1.at[q], images.at[q, k], send_image.at[q, k], recv_image.at[q, k], partner(k, -1))

    def part_copy(q, k):
        return copy(part1.at[q, rep], part1.at[q, rep], send1.at[q, k], recv1.at[q, k], rep_peer(k))

    @pl.when(own_first)
    def _():
        pl.semaphore_wait(barrier, REPS + 1)
        packets[0] = packet[...]

    @pl.when(not_own)
    def _():
        pl.semaphore_wait(barrier, REPS + 2)
        first_copy().start()

    own_aug[...] = augmented(packet[...], True).astype(BF16)

    def rows(k):
        return pl.ds(pl.multiple_of(k * BLOCK, BLOCK), BLOCK)

    def held(k, q):
        return pl.ds(pl.multiple_of((q * NEAR + k) * WIDTH, WIDTH), WIDTH)

    def fetch(k):
        @pl.when(jnp.logical_not(jnp.logical_and(own_first, k == 0)))
        def _():
            copy(packets.at[k], packets.at[k], send_near.at[k], recv_near.at[k], rep_peer(1)).wait_recv()

        @pl.when(k < NEAR - 2)
        def _():
            ring_copy(k).start()

        @pl.when(k == 0)
        def _():
            turn_copy().start()

        remote_aug[rows(k), :] = augmented(packets[k], False).astype(BF16).T

    def values(dist):
        dist = jnp.maximum(dist, TINY)
        t = dist * lax.rsqrt(dist)
        value = ((t + LINEAR) * t + CONST) * jnp.exp2(-t)
        lead = value.astype(BF16)
        return lead, (value - lead.astype(F32)).astype(BF16)

    def build_whole(k, total):
        vector = two_terms(packets[k, 4:8] * OUTER)
        lead, rest = values(matmul(remote_aug[rows(k), :], own_aug[...]))
        for q in range(PARTS):
            high[held(k, q), :] = lead[q * WIDTH:(q + 1) * WIDTH]
            low[held(k, q), :] = rest[q * WIDTH:(q + 1) * WIDTH]
        fetch(k + 1)
        return total + matmul(vector, lead) + matmul(vector, rest)

    zeros = jnp.zeros((16, BLOCK), F32)
    fetch(jnp.int32(0))
    partial[...] = lax.fori_loop(0, WHOLE, build_whole, zeros)
    for k in range(WHOLE + 1, NEAR):
        fetch(jnp.int32(k))

    def image_part(q):
        for k in range(1, REPS):
            part_copy(q, k).wait_recv()
        whole = part1[q, 0]
        for other in range(1, REPS):
            whole = whole + part1[q, other]
        cols = pl.ds(pl.multiple_of(q * WIDTH, WIDTH), WIDTH)
        image1[q] = whole + noise[:, cols] * right[:, cols]

        for k in range(NEAR - 1, 0, -1):
            image_copy(q, k).start()

        @pl.when(own_first)
        def _():
            images[q, 0] = image1[q]

        @pl.when(not_own)
        def _():
            image_copy(q, 0).start()

    def build_part(q, _):
        cols = pl.ds(pl.multiple_of(q * WIDTH, WIDTH), WIDTH)
        total = partial[:, cols]
        own = own_aug[:, cols]
        for k in range(WHOLE, NEAR):
            vector = two_terms(packets[k, 4:8] * OUTER)
            lead, rest = values(matmul(remote_aug[rows(k), :], own))
            for part in range(PARTS):
                high[held(k, part), cols] = lead[part * WIDTH:(part + 1) * WIDTH]
                low[held(k, part), cols] = rest[part * WIDTH:(part + 1) * WIDTH]
            total = total + matmul(vector, lead) + matmul(vector, rest)
        part1[q, rep] = total[0:4] + total[4:8]
        for k in range(1, REPS):
            part_copy(q, k).start()

        return 0

    lax.fori_loop(0, PARTS, build_part, 0)
    for q in range(PARTS):
        image_part(q)

    def again(n, total):
        q, first = n // 2, n % 2 * 4

        @pl.when(jnp.logical_not(jnp.logical_and(own_first, first == 0)))
        def _():
            arrived(q, first)

        for k in range(1, 4):
            arrived(q, first + k)
        vector = two_terms(jnp.concatenate([images[q, first + k] for k in range(4)], axis=1) * OUTER)
        part = rows(n)
        return total + matmul(vector, high[part, :]) + matmul(vector, low[part, :])

    def arrived(q, k):
        copy(images.at[q, k], images.at[q, k], send_image.at[q, k], recv_image.at[q, k], rep_peer(1)).wait_recv()

    total = lax.fori_loop(0, 2 * PARTS, again, zeros)
    own_part = total[0:4] + total[4:8]
    r0 = right[...]
    w1 = jnp.concatenate([image1[q] for q in range(PARTS)], axis=1)
    spread = noise[...] * w1

    lane = lax.broadcasted_iota(jnp.int32, (4, 128), 1)
    once = jnp.where(rep == 0, 1.0, 0.0)
    mine = own_part + once * spread
    grams = jnp.zeros((4, 128), F32)
    for at, product in enumerate((once * r0 * r0, once * r0 * w1, once * w1 * w1, r0 * mine, w1 * mine)):
        grams = jnp.where(lane == at, jnp.sum(product, axis=1, keepdims=True), grams)

    def over(slots, me, stage, peer, value):
        slots[me] = value
        copies = [
            copy(slots.at[me], slots.at[me], send_end.at[stage, k], recv_end.at[stage, k], peer(k)) for k in range(1, 8)
        ]
        for one in copies:
            one.start()
        return copies

    def added(slots, copies):
        for one in copies:
            one.wait_recv()
        value = slots[0]
        for other in range(1, 8):
            value = value + slots[other]
        return value

    across = lax.axis_index("blk") % 8
    first = over(sums_rep, rep, 0, rep_peer, grams)
    bulk = over(part2, rep, 3, rep_peer, own_part)
    @pl.when(not_own)
    def _():
        first_copy().wait_send()

    turn_copy().wait_send()
    for k in range(NEAR - 2):
        ring_copy(k).wait_send()
    def left(q, _):
        @pl.when(not_own)
        def _():
            image_copy(q, 0).wait_send()

        for k in range(1, NEAR):
            image_copy(q, k).wait_send()
        for k in range(1, REPS):
            part_copy(q, k).wait_send()
        return 0

    lax.fori_loop(0, PARTS, left, 0)

    second = over(sums_y, y, 1, y_peer, added(sums_rep, first))
    third = over(sums_zx, across, 2, zx_peer, added(sums_y, second))
    w2 = added(part2, bulk) + spread
    for one in first + bulk + second:
        one.wait_send()
    grams = added(sums_zx, third)

    g00, g01, g11, g02, g12 = (grams[:, at:at + 1] for at in range(5))
    alpha = g00 / g01
    new = g00 - 2.0 * alpha * g01 + alpha * alpha * g11
    more = 1.0 + new / g00
    bottom = more * more * g01 - alpha * more * (g02 + g11) + alpha * alpha * g12
    alpha2 = new / bottom
    direction = more * r0 - alpha * w1
    image = more * w1 - alpha * w2
    out[0:4] = alpha * r0 + alpha2 * direction
    out[4:8] = (r0 - alpha * w1) - alpha2 * image
    for one in third:
        one.wait_send()


def local(coords, noise, right_side):
    vmem = pl.BlockSpec(memory_space=pltpu.VMEM)
    field = jax.ShapeDtypeStruct((8, BLOCK), F32)
    call = pl.pallas_call(
        kernel,
        out_shape=field,
        in_specs=[pl.BlockSpec(memory_space=pl.ANY)] * 3,
        out_specs=vmem,
        scratch_shapes=[
            pltpu.VMEM((8, BLOCK), F32),
            pltpu.VMEM((NEAR, 8, BLOCK), F32),
            pltpu.VMEM((NEAR * BLOCK, BLOCK), BF16),
            pltpu.VMEM((NEAR * BLOCK, BLOCK), BF16),
            pltpu.VMEM((128, BLOCK), BF16),
            pltpu.VMEM((NEAR * BLOCK, 128), BF16),
            pltpu.VMEM((16, BLOCK), F32),
            pltpu.VMEM((PARTS, REPS, 4, WIDTH), F32),
            pltpu.VMEM((PARTS, 4, WIDTH), F32),
            pltpu.VMEM((PARTS, NEAR, 4, WIDTH), F32),
            pltpu.VMEM((REPS, 4, BLOCK), F32),
            pltpu.VMEM((REPS, 4, 128), F32),
            pltpu.VMEM((8, 4, 128), F32),
            pltpu.VMEM((8, 4, 128), F32),
            pltpu.SemaphoreType.DMA((NEAR,)),
            pltpu.SemaphoreType.DMA((NEAR,)),
            pltpu.SemaphoreType.DMA((PARTS, REPS)),
            pltpu.SemaphoreType.DMA((PARTS, REPS)),
            pltpu.SemaphoreType.DMA((PARTS, NEAR)),
            pltpu.SemaphoreType.DMA((PARTS, NEAR)),
            pltpu.SemaphoreType.DMA((4, 8)),
            pltpu.SemaphoreType.DMA((4, 8)),
            pltpu.VMEM((3, BLOCK), F32),
            pltpu.VMEM((1, BLOCK), F32),
            pltpu.VMEM((4, BLOCK), F32),
            pltpu.SemaphoreType.DMA((3,)),
        ],
        compiler_params=pltpu.CompilerParams(
            collective_id=0, has_side_effects=True, vmem_limit_bytes=60 * 1024 * 1024
        ),
    )
    both = call(coords, noise[None, :], right_side)
    return both[0:4], both[4:8]


def solution(mesh):
    return jax.shard_map(
        local,
        mesh=mesh,
        in_specs=(P(None, "blk"), P("blk"), P(None, "blk")),
        out_specs=(P(None, "blk"), P(None, "blk")),
        check_vma=False,
    )
```
